32 devices in a mesh: parts: 2 (over y), chan: 4 (over z), grp: 2 (over x), tpl: 2 (over core).
Axes of the slice: x: 2, y: 2, z: 4, core: 2. Of those that a mesh axis runs over, the one named last changes fastest.
Arguments:
- records: bfloat16 [64, 32768], P(None, ('parts', 'chan', 'grp')), parts along dimension 1, may hold values from -54 to 54
- fir: bfloat16 [32], replicated, may hold values from -1 to 1
- templates: bfloat16 [48, 64, 128], P('tpl', ('chan', 'grp')), may hold values from -0.09375 to 0.09375
- channel_sel: int32 [48, 64], P('tpl', ('chan', 'grp')), may hold values 0 or 1
- moveout: int32 [48, 64], P('tpl', ('chan', 'grp')), may hold values from 0 to 127
- alive: int32 [64], P(('chan', 'grp')), may hold values 0 or 1
Outputs:
- stack: float32 [48, 32768], P('tpl', ('parts', 'chan')), parts along dimension 1
The draws below stay inside these ranges and needn't reach their ends.
There are 2 independent parts, one for each index of `parts`. The reference program is written for one: setup_inputs(seed, part) draws one part's arguments, and reference() takes and returns one part's arrays. A program takes and returns all parts, laid end to end along the dimension named above; an argument that names none is the same for every part. Nothing has to cross between parts.
All inputs are finite; a program needn't handle non-finite values. No bound on the sum of `channel_sel` or of `alive` on one device may be relied on, other than what follows from the above.
Results may differ from the reference program's by a relative error of at most 0.0029.
Values may be sent and summed in bfloat16 or wider, within the bound.
A program may use at most 64 MiB of HBM per device.

```python
import math
import jax
import jax.numpy as jnp
from jax import lax

S = 16384
K = 48
L = 128
MMAX = 128
FT = 32
CH = 64


def draw_records(key, part):
    key_noise, key_chan, key_time = jax.random.split(key, 3)
    block_count = S // 256
    noise = jnp.clip(jax.random.normal(key_noise, (CH, S), jnp.float32), -6.0, 6.0)
    chan_scale = jnp.exp(jax.random.uniform(key_chan, (CH, 1), jnp.float32, minval=math.log(0.3), maxval=math.log(3.0)))
    block_scale = jnp.exp(jax.random.uniform(key_time, (1, block_count), jnp.float32, minval=math.log(0.3), maxval=math.log(3.0)))
    time_scale = jnp.repeat(block_scale, 256, axis=1)
    return (noise * chan_scale * time_scale).astype(jnp.bfloat16)


def with_ends(values, stream_key, low, largest):
    spot = [jax.random.randint(jax.random.fold_in(stream_key, axis), (), 0, length) for axis, length in enumerate(values.shape)]
    main_axis = values.shape.index(max(values.shape))
    neighbour = spot[:main_axis] + [(spot[main_axis] + 1) % values.shape[main_axis]] + spot[main_axis + 1:]
    return values.at[tuple(spot)].set(low).at[tuple(neighbour)].set(largest)


def levels(key, dims, cuts, low, high):
    def one(dim, blocks):
        heights = jax.random.uniform(jax.random.fold_in(jax.random.fold_in(key, 6), dim), (blocks,), jnp.float32, low / len(cuts), high / len(cuts))
        return jnp.repeat(jnp.exp(heights), dims[dim] // blocks).reshape((-1,) + (1,) * (len(dims) - dim - 1))

    factor_of = one(*cuts[0])
    for cut in cuts[1:]:
        factor_of = factor_of * one(*cut)
    return factor_of


def scatter_about(own_key, shape, width, most, cuts=(), kind=jnp.bfloat16):
    factor_of = levels(own_key, shape, cuts, -0.22, 0.18) if cuts else 1.0
    values = jax.random.normal(own_key, shape, jnp.float32) * width * factor_of
    return jnp.minimum(jnp.maximum(values, -most), most).astype(kind)


def setup_inputs(seed: int = 0, part: int = 0) -> dict:
    streams_of = jax.random.split(jax.random.key(seed), 7)
    own_keys = jax.random.split(jax.random.fold_in(streams_of[6], part), 7)
    records = draw_records(jax.random.fold_in(jax.random.fold_in(streams_of[6], part), 71), part)
    fir = scatter_about(streams_of[1], (FT,), FT ** -0.5, 1.0)
    templates = scatter_about(streams_of[2], (K, CH, L), (CH * L // 2) ** -0.5, 0.09375, ((0, 2), (1, 8)))
    channel_sel = with_ends((jax.random.randint(streams_of[3], (K, CH), 0, 2) < 1).astype(jnp.int32), jax.random.fold_in(streams_of[3], 1), 0, 1)
    moveout = with_ends(jax.random.randint(streams_of[4], (K, CH), 0, MMAX), jax.random.fold_in(streams_of[4], 1), 0, MMAX - 1).astype(jnp.int32)
    alive = with_ends((jax.random.randint(streams_of[5], (CH,), 0, 8) < 7).astype(jnp.int32), jax.random.fold_in(streams_of[5], 1), 0, 1)
    return {"records": records, "fir": fir, "templates": templates, "channel_sel": channel_sel, "moveout": moveout, "alive": alive}


def reference(records, fir, templates, channel_sel, moveout, alive):
    signal = records.astype(jnp.float32)
    tap_values = fir.astype(jnp.float32)
    filtered = jnp.zeros(signal.shape, jnp.float32)
    for lag_index in range(FT):
        shifted = jnp.pad(signal, ((0, 0), (lag_index, 0)))[:, :S]
        filtered = filtered + tap_values[lag_index] * shifted
    power = lax.optimization_barrier(jnp.mean(filtered * filtered, axis=1, keepdims=True))
    whitened = (filtered * lax.rsqrt(power + 1e-06)).astype(jnp.bfloat16)
    keep_mask = (channel_sel * alive[None, :]).astype(jnp.bfloat16)
    weighted = templates * keep_mask[:, :, None]
    extended = L + MMAX
    fft_length = S + extended
    spectrum = jnp.fft.rfft(whitened.astype(jnp.float32), n=fft_length, axis=1)

    def one_template(operands):
        weight_rows, shift_rows = operands
        lags = jnp.arange(extended, dtype=jnp.int32)[None, :] - shift_rows[:, None]
        inside = (lags >= 0) & (lags < L)
        picked = jnp.take_along_axis(weight_rows, jnp.clip(lags, 0, L - 1), axis=1)
        shifted_tpl = jnp.where(inside, picked.astype(jnp.float32), jnp.zeros((), jnp.float32))
        tpl_spectrum = jnp.fft.rfft(shifted_tpl, n=fft_length, axis=1)
        product = lax.optimization_barrier(jnp.sum(spectrum * jnp.conj(tpl_spectrum), axis=0))
        return jnp.fft.irfft(product, n=fft_length)[:S].astype(jnp.float32)
    return lax.map(one_template, (weighted, moveout))
```

```python
import jax
import jax.numpy as jnp
from jax import lax
from jax.sharding import PartitionSpec as P

axes = ("chan", "grp")
stride = 8
extended = 256
lags = extended + stride
small_eps = 1e-06
group_rows = 64


def filter_matrix(fir):
    lag = jnp.arange(128)[None, :] + 128 - jnp.arange(256)[:, None]
    hits = lag[:, :, None] == jnp.arange(fir.shape[0])[None, None, :]
    return jnp.sum(jnp.where(hits, fir.astype(jnp.float32), 0.0), axis=2).astype(jnp.bfloat16)


def shift_templates(templates, channel_sel, moveout, alive):
    keep = (channel_sel * alive[None, :]).astype(jnp.bfloat16)
    rows = jnp.pad(templates * keep[:, :, None], ((0, 0), (0, 0), (0, 128)))
    for bit in range(7):
        moved = jnp.pad(rows, ((0, 0), (0, 0), (1 << bit, 0)))[:, :, :extended]
        rows = jnp.where(((moveout >> bit) & 1)[:, :, None] == 1, moved, rows)
    return rows


def time_split(records, fir, templates, channel_sel, moveout, alive, chan, grp):
    chans, length = records.shape
    count = chan * grp
    me = lax.axis_index(axes)
    before = lax.ppermute(records[:, length - 128:], axes, [(i, i + 1) for i in range(count - 1)])
    after = lax.ppermute(records[:, :extended], axes, [(i + 1, i) for i in range(count - 1)])
    shifted = shift_templates(templates, channel_sel, moveout, alive)
    shifted = lax.all_gather(shifted, axes, axis=1, tiled=True)
    signal = jnp.concatenate([before, records, after], axis=1)
    total = length + extended
    blocks = signal.reshape(chans, total // 128 + 1, 128)
    paired = jnp.concatenate([blocks[:, :-1], blocks[:, 1:]], axis=2)
    filtered = jnp.einsum("cbi,ir->cbr", paired, filter_matrix(fir), preferred_element_type=jnp.float32)
    filtered = filtered.reshape(chans, total)
    own = filtered[:, :length]
    power = lax.psum(jnp.sum(own * own, axis=1, keepdims=True), axes) / (length * count)
    inside = (jnp.arange(total) < length) | (me < count - 1)
    whitened = jnp.where(inside[None], filtered * lax.rsqrt(power + small_eps), 0.0).astype(jnp.bfloat16)
    steps = length // stride

    def part(wave, tpl):
        cells = wave.reshape(wave.shape[0], total // stride, stride)
        left = jnp.stack([cells[:, j:j + steps] for j in range(lags // stride)], axis=1)
        right = jnp.stack([jnp.pad(tpl, ((0, 0), (0, 0), (r, stride - r))) for r in range(stride)])
        right = right.reshape(stride, tpl.shape[0], tpl.shape[1], lags // stride, stride)
        return jnp.einsum("cjbs,rkcjs->kbr", left, right, preferred_element_type=jnp.float32)

    groups = chans // group_rows
    if groups == 1:
        stack = part(whitened, shifted)
    else:
        waves = whitened.reshape(groups, group_rows, total)
        tpls = shifted.reshape(-1, groups, group_rows, extended).transpose(1, 0, 2, 3)
        stack = jnp.zeros((shifted.shape[0], steps, stride), jnp.float32)
        stack = lax.scan(lambda acc, x: (acc + part(*x), None), stack, (waves, tpls))[0]
    stack = stack.reshape(shifted.shape[0], length)
    return lax.all_gather(stack, "grp", axis=1, tiled=True)


def solution(mesh):
    chan, grp = mesh.shape["chan"], mesh.shape["grp"]

    def body(*args):
        return time_split(*args, chan, grp)

    in_specs = (
        P(None, ("parts", "chan", "grp")),
        P(),
        P("tpl", ("chan", "grp"), None),
        P("tpl", ("chan", "grp")),
        P("tpl", ("chan", "grp")),
        P(("chan", "grp")),
    )
    out_specs = P("tpl", ("parts", "chan"))
    return jax.shard_map(body, mesh=mesh, in_specs=in_specs, out_specs=out_specs, check_vma=False)
```

```python
import functools

import jax
import jax.numpy as jnp
from jax import lax
from jax.experimental import pallas as pl
from jax.experimental.pallas import tpu as pltpu
from jax.sharding import PartitionSpec as P

axes = ("chan", "grp")
stride = 8
extended = 256
lags = extended + stride
small_eps = 1e-06
group_rows = 64


def filter_matrix(fir):
    lag = jnp.arange(128)[None, :] + 128 - jnp.arange(256)[:, None]
    hits = lag[:, :, None] == jnp.arange(fir.shape[0])[None, None, :]
    return jnp.sum(jnp.where(hits, fir.astype(jnp.float32), 0.0), axis=2).astype(jnp.bfloat16)


def shift_templates(templates, channel_sel, moveout, alive):
    keep = (channel_sel * alive[None, :]).astype(jnp.bfloat16)
    rows = jnp.pad(templates * keep[:, :, None], ((0, 0), (0, 0), (0, 128)))
    for bit in range(7):
        moved = jnp.pad(rows, ((0, 0), (0, 0), (1 << bit, 0)))[:, :, :extended]
        rows = jnp.where(((moveout >> bit) & 1)[:, :, None] == 1, moved, rows)
    return rows


def gather_kernel(grp, count, tpl_ref, sum_ref, tpl_all, sum_all, send_sem, recv_sem, own_sem):
    me = lax.axis_index("chan") * grp + lax.axis_index("grp")

    def place(index):
        return {"chan": index // grp, "grp": index % grp}

    barrier = pltpu.get_barrier_semaphore()
    for step in range(1, count):
        pl.semaphore_signal(barrier, inc=1, device_id=place((me + step) % count), device_id_type=pl.DeviceIdType.MESH)
    pl.semaphore_wait(barrier, count - 1)
    sent = []
    for kind, (src, dst) in enumerate(((sum_ref, sum_all), (tpl_ref, tpl_all))):
        for step in range(1, count):
            sent.append(pltpu.make_async_remote_copy(
                src_ref=src,
                dst_ref=dst.at[me],
                send_sem=send_sem.at[kind, step],
                recv_sem=recv_sem.at[kind, step],
                device_id=place((me + step) % count),
                device_id_type=pl.DeviceIdType.MESH,
            ))
            sent[-1].start()
        kept = pltpu.make_async_copy(src, dst.at[me], own_sem.at[kind])
        kept.start()
        kept.wait()
    for copy in sent:
        copy.wait()


def gather(tpl, sums, grp, count):
    return pl.pallas_call(
        functools.partial(gather_kernel, grp, count),
        out_shape=(
            jax.ShapeDtypeStruct((count,) + tpl.shape, tpl.dtype),
            jax.ShapeDtypeStruct((count,) + sums.shape, sums.dtype),
        ),
        in_specs=[pl.BlockSpec(memory_space=pltpu.VMEM)] * 2,
        out_specs=[pl.BlockSpec(memory_space=pltpu.VMEM)] * 2,
        scratch_shapes=[
            pltpu.SemaphoreType.DMA((2, count)),
            pltpu.SemaphoreType.DMA((2, count)),
            pltpu.SemaphoreType.DMA((2,)),
        ],
        compiler_params=pltpu.CompilerParams(collective_id=0, has_side_effects=True, vmem_limit_bytes=24 << 20),
    )(tpl, sums)


def correlate_kernel(wave_ref, tpl_ref, out_ref):
    steps = out_ref.shape[0]
    width = wave_ref.shape[1]
    total = jnp.zeros(out_ref.shape, jnp.float32)
    for j in range(lags // stride):
        left = wave_ref[j:j + steps, :].astype(jnp.bfloat16)
        start = width * (j + 1)
        right = jnp.concatenate(
            [tpl_ref[:, start - 128 * r:start - 128 * r + width] for r in range(stride // 2)], axis=0
        )
        total = total + lax.dot_general(left, right, (((1,), (1,)), ((), ())), preferred_element_type=jnp.float32)
    out_ref[...] = total


def packed(records, fir, templates, channel_sel, moveout, alive, chan, grp):
    chans, length = records.shape
    tpl_count = templates.shape[0]
    count = chan * grp
    me = lax.axis_index(axes)
    before = lax.ppermute(records[:, length - 128:], axes, [(i, i + 1) for i in range(count - 1)])
    after = lax.ppermute(records[:, :extended], axes, [(i + 1, i) for i in range(count - 1)])
    shifted = shift_templates(templates, channel_sel, moveout, alive)
    signal = jnp.concatenate([before, records, after], axis=1)
    total = length + extended
    blocks = signal.reshape(chans, total // 128 + 1, 128)
    paired = jnp.concatenate([blocks[:, :-1], blocks[:, 1:]], axis=2)
    filtered = jnp.einsum("cbi,ir->cbr", paired, filter_matrix(fir), preferred_element_type=jnp.float32)
    filtered = filtered.reshape(chans, total)
    own = filtered[:, :length]
    sums = jnp.broadcast_to(jnp.pad(jnp.sum(own * own, axis=1), (0, 128 - chans))[None], (8, 128))
    rows = shifted.reshape(-1, extended)
    tpl_all, sum_all = gather(rows, sums, grp, count)
    power = jnp.sum(sum_all[:, 0, :chans], axis=0)[:, None] / (length * count)
    inside = (jnp.arange(total) < length) | (me < count - 1)
    whitened = jnp.where(inside[None], filtered * lax.rsqrt(power + small_eps), 0.0).astype(jnp.bfloat16)
    wave = whitened.astype(jnp.float32).T.reshape(total // stride, stride * chans)
    tpl = tpl_all.reshape(count, tpl_count, chans // count, extended).transpose(1, 3, 0, 2)
    tpl = jnp.pad(tpl.reshape(tpl_count, extended * chans), ((0, 32 - tpl_count), (0, 0)))
    room = stride * chans
    tpl = jnp.concatenate(
        [jnp.pad(tpl, ((0, 0), (room, room))), jnp.pad(tpl, ((0, 0), (room + chans, room - chans)))], axis=0
    )
    steps = length // stride
    out = pl.pallas_call(
        correlate_kernel,
        out_shape=jax.ShapeDtypeStruct((steps, 32 * stride), jnp.float32),
        in_specs=[pl.BlockSpec(memory_space=pltpu.VMEM)] * 2,
        out_specs=pl.BlockSpec(memory_space=pltpu.VMEM),
        compiler_params=pltpu.CompilerParams(vmem_limit_bytes=32 << 20),
    )(wave, tpl)
    stack = out.reshape(steps, stride, 32)[:, :, :tpl_count].transpose(2, 0, 1).reshape(tpl_count, length)
    other = lax.ppermute(stack, "grp", [(0, 1), (1, 0)])
    first = lax.axis_index("grp") == 0
    return jnp.concatenate([jnp.where(first, stack, other), jnp.where(first, other, stack)], axis=1)


def time_split(records, fir, templates, channel_sel, moveout, alive, chan, grp):
    chans, length = records.shape
    count = chan * grp
    me = lax.axis_index(axes)
    before = lax.ppermute(records[:, length - 128:], axes, [(i, i + 1) for i in range(count - 1)])
    after = lax.ppermute(records[:, :extended], axes, [(i + 1, i) for i in range(count - 1)])
    shifted = shift_templates(templates, channel_sel, moveout, alive)
    shifted = lax.all_gather(shifted, axes, axis=1, tiled=True)
    signal = jnp.concatenate([before, records, after], axis=1)
    total = length + extended
    blocks = signal.reshape(chans, total // 128 + 1, 128)
    paired = jnp.concatenate([blocks[:, :-1], blocks[:, 1:]], axis=2)
    filtered = jnp.einsum("cbi,ir->cbr", paired, filter_matrix(fir), preferred_element_type=jnp.float32)
    filtered = filtered.reshape(chans, total)
    own = filtered[:, :length]
    power = lax.psum(jnp.sum(own * own, axis=1, keepdims=True), axes) / (length * count)
    inside = (jnp.arange(total) < length) | (me < count - 1)
    whitened = jnp.where(inside[None], filtered * lax.rsqrt(power + small_eps), 0.0).astype(jnp.bfloat16)
    steps = length // stride

    def part(wave, tpl):
        cells = wave.reshape(wave.shape[0], total // stride, stride)
        left = jnp.stack([cells[:, j:j + steps] for j in range(lags // stride)], axis=1)
        right = jnp.stack([jnp.pad(tpl, ((0, 0), (0, 0), (r, stride - r))) for r in range(stride)])
        right = right.reshape(stride, tpl.shape[0], tpl.shape[1], lags // stride, stride)
        return jnp.einsum("cjbs,rkcjs->kbr", left, right, preferred_element_type=jnp.float32)

    groups = chans // group_rows
    if groups == 1:
        stack = part(whitened, shifted)
    else:
        waves = whitened.reshape(groups, group_rows, total)
        tpls = shifted.reshape(-1, groups, group_rows, extended).transpose(1, 0, 2, 3)
        stack = jnp.zeros((shifted.shape[0], steps, stride), jnp.float32)
        stack = lax.scan(lambda acc, x: (acc + part(*x), None), stack, (waves, tpls))[0]
    stack = stack.reshape(shifted.shape[0], length)
    return lax.all_gather(stack, "grp", axis=1, tiled=True)


def solution(mesh):
    chan, grp = mesh.shape["chan"], mesh.shape["grp"]

    def body(*args):
        chans, tpl_count = args[0].shape[0], args[2].shape[0]
        if chans == 64 and tpl_count <= 32 and grp == 2:
            return packed(*args, chan, grp)
        return time_split(*args, chan, grp)

    in_specs = (
        P(None, ("parts", "chan", "grp")),
        P(),
        P("tpl", ("chan", "grp"), None),
        P("tpl", ("chan", "grp")),
        P("tpl", ("chan", "grp")),
        P(("chan", "grp")),
    )
    out_specs = P("tpl", ("parts", "chan"))
    return jax.shard_map(body, mesh=mesh, in_specs=in_specs, out_specs=out_specs, check_vma=False)
```

```python
import functools

import jax
import jax.numpy as jnp
from jax import lax
from jax.experimental import pallas as pl
from jax.experimental.pallas import tpu as pltpu
from jax.sharding import PartitionSpec as P

axes = ("chan", "grp")
stride = 8
extended = 256
lags = extended + stride
small_eps = 1e-06
group_rows = 64


def filter_matrix(fir):
    lag = jnp.arange(128)[None, :] + 128 - jnp.arange(256)[:, None]
    hits = lag[:, :, None] == jnp.arange(fir.shape[0])[None, None, :]
    return jnp.sum(jnp.where(hits, fir.astype(jnp.float32), 0.0), axis=2).astype(jnp.bfloat16)


def shift_templates(templates, channel_sel, moveout, alive):
    keep = (channel_sel * alive[None, :]).astype(jnp.bfloat16)
    rows = jnp.pad(templates * keep[:, :, None], ((0, 0), (0, 0), (0, 128)))
    for bit in range(7):
        moved = jnp.pad(rows, ((0, 0), (0, 0), (1 << bit, 0)))[:, :, :extended]
        rows = jnp.where(((moveout >> bit) & 1)[:, :, None] == 1, moved, rows)
    return rows


def gather_kernel(grp, count, tpl_ref, sum_ref, tpl_all, sum_all, send_sem, recv_sem, own_sem):
    me = lax.axis_index("chan") * grp + lax.axis_index("grp")

    def place(index):
        return {"chan": index // grp, "grp": index % grp}

    barrier = pltpu.get_barrier_semaphore()
    for step in range(1, count):
        pl.semaphore_signal(barrier, inc=1, device_id=place((me + step) % count), device_id_type=pl.DeviceIdType.MESH)
    pl.semaphore_wait(barrier, count - 1)
    sent = []
    for kind, (src, dst) in enumerate(((sum_ref, sum_all), (tpl_ref, tpl_all))):
        for step in range(1, count):
            sent.append(pltpu.make_async_remote_copy(
                src_ref=src,
                dst_ref=dst.at[me],
                send_sem=send_sem.at[kind, step],
                recv_sem=recv_sem.at[kind, step],
                device_id=place((me + step) % count),
                device_id_type=pl.DeviceIdType.MESH,
            ))
            sent[-1].start()
        kept = pltpu.make_async_copy(src, dst.at[me], own_sem.at[kind])
        kept.start()
        kept.wait()
    for copy in sent:
        copy.wait()


def gather(tpl, sums, grp, count):
    return pl.pallas_call(
        functools.partial(gather_kernel, grp, count),
        out_shape=(
            jax.ShapeDtypeStruct((count,) + tpl.shape, tpl.dtype),
            jax.ShapeDtypeStruct((count,) + sums.shape, sums.dtype),
        ),
        in_specs=[pl.BlockSpec(memory_space=pltpu.VMEM)] * 2,
        out_specs=[pl.BlockSpec(memory_space=pltpu.VMEM)] * 2,
        scratch_shapes=[
            pltpu.SemaphoreType.DMA((2, count)),
            pltpu.SemaphoreType.DMA((2, count)),
            pltpu.SemaphoreType.DMA((2,)),
        ],
        compiler_params=pltpu.CompilerParams(collective_id=0, has_side_effects=True, vmem_limit_bytes=24 << 20),
    )(tpl, sums)


def correlate_kernel(wave_ref, tpl_ref, out_ref):
    steps = out_ref.shape[0]
    width = wave_ref.shape[1]
    total = jnp.zeros(out_ref.shape, jnp.float32)
    for j in range(lags // stride):
        left = wave_ref[j:j + steps, :].astype(jnp.bfloat16)
        start = width * (j + 1)
        right = jnp.concatenate(
            [tpl_ref[:, start - 128 * r:start - 128 * r + width] for r in range(stride // 2)], axis=0
        )
        total = total + lax.dot_general(left, right, (((1,), (1,)), ((), ())), preferred_element_type=jnp.float32)
    out_ref[...] = total


def packed(records, fir, templates, channel_sel, moveout, alive, chan, grp):
    chans, length = records.shape
    tpl_count = templates.shape[0]
    count = chan * grp
    me = lax.axis_index(axes)
    before = lax.ppermute(records[:, length - 128:], axes, [(i, i + 1) for i in range(count - 1)])
    after = lax.ppermute(records[:, :extended], axes, [(i + 1, i) for i in range(count - 1)])
    shifted = shift_templates(templates, channel_sel, moveout, alive)
    signal = jnp.concatenate([before, records, after], axis=1)
    total = length + extended
    blocks = signal.reshape(chans, total // 128 + 1, 128)
    paired = jnp.concatenate([blocks[:, :-1], blocks[:, 1:]], axis=2)
    filtered = jnp.einsum("cbi,ir->cbr", paired, filter_matrix(fir), preferred_element_type=jnp.float32)
    filtered = filtered.reshape(chans, total)
    own = filtered[:, :length]
    sums = jnp.broadcast_to(jnp.pad(jnp.sum(own * own, axis=1), (0, 128 - chans))[None], (8, 128))
    rows = shifted.reshape(-1, extended)
    tpl_all, sum_all = gather(rows, sums, grp, count)
    power = jnp.sum(sum_all[:, 0, :chans], axis=0)[:, None] / (length * count)
    inside = (jnp.arange(total) < length) | (me < count - 1)
    whitened = jnp.where(inside[None], filtered * lax.rsqrt(power + small_eps), 0.0).astype(jnp.bfloat16)
    wave = whitened.astype(jnp.float32).T.reshape(total // stride, stride * chans)
    tpl = tpl_all.reshape(count, tpl_count, chans // count, extended).transpose(1, 3, 0, 2)
    tpl = jnp.pad(tpl.reshape(tpl_count, extended * chans), ((0, 32 - tpl_count), (0, 0)))
    room = stride * chans
    tpl = jnp.concatenate(
        [jnp.pad(tpl, ((0, 0), (room, room))), jnp.pad(tpl, ((0, 0), (room + chans, room - chans)))], axis=0
    )
    steps = length // stride
    out = pl.pallas_call(
        correlate_kernel,
        out_shape=jax.ShapeDtypeStruct((steps, 32 * stride), jnp.float32),
        in_specs=[pl.BlockSpec(memory_space=pltpu.VMEM)] * 2,
        out_specs=pl.BlockSpec(memory_space=pltpu.VMEM),
        compiler_params=pltpu.CompilerParams(vmem_limit_bytes=32 << 20),
    )(wave, tpl)
    stack = out.reshape(steps, stride, 32)[:, :, :tpl_count].transpose(2, 0, 1).reshape(tpl_count, length)
    other = lax.ppermute(stack, "grp", [(0, 1), (1, 0)])
    first = lax.axis_index("grp") == 0
    return jnp.where(
        first, jnp.concatenate([stack, other], axis=1), jnp.concatenate([other, stack], axis=1)
    )


def time_split(records, fir, templates, channel_sel, moveout, alive, chan, grp):
    chans, length = records.shape
    count = chan * grp
    me = lax.axis_index(axes)
    before = lax.ppermute(records[:, length - 128:], axes, [(i, i + 1) for i in range(count - 1)])
    after = lax.ppermute(records[:, :extended], axes, [(i + 1, i) for i in range(count - 1)])
    shifted = shift_templates(templates, channel_sel, moveout, alive)
    shifted = lax.all_gather(shifted, axes, axis=1, tiled=True)
    signal = jnp.concatenate([before, records, after], axis=1)
    total = length + extended
    blocks = signal.reshape(chans, total // 128 + 1, 128)
    paired = jnp.concatenate([blocks[:, :-1], blocks[:, 1:]], axis=2)
    filtered = jnp.einsum("cbi,ir->cbr", paired, filter_matrix(fir), preferred_element_type=jnp.float32)
    filtered = filtered.reshape(chans, total)
    own = filtered[:, :length]
    power = lax.psum(jnp.sum(own * own, axis=1, keepdims=True), axes) / (length * count)
    inside = (jnp.arange(total) < length) | (me < count - 1)
    whitened = jnp.where(inside[None], filtered * lax.rsqrt(power + small_eps), 0.0).astype(jnp.bfloat16)
    steps = length // stride

    def part(wave, tpl):
        cells = wave.reshape(wave.shape[0], total // stride, stride)
        left = jnp.stack([cells[:, j:j + steps] for j in range(lags // stride)], axis=1)
        right = jnp.stack([jnp.pad(tpl, ((0, 0), (0, 0), (r, stride - r))) for r in range(stride)])
        right = right.reshape(stride, tpl.shape[0], tpl.shape[1], lags // stride, stride)
        return jnp.einsum("cjbs,rkcjs->kbr", left, right, preferred_element_type=jnp.float32)

    groups = chans // group_rows
    if groups == 1:
        stack = part(whitened, shifted)
    else:
        waves = whitened.reshape(groups, group_rows, total)
        tpls = shifted.reshape(-1, groups, group_rows, extended).transpose(1, 0, 2, 3)
        stack = jnp.zeros((shifted.shape[0], steps, stride), jnp.float32)
        stack = lax.scan(lambda acc, x: (acc + part(*x), None), stack, (waves, tpls))[0]
    stack = stack.reshape(shifted.shape[0], length)
    return lax.all_gather(stack, "grp", axis=1, tiled=True)


def solution(mesh):
    chan, grp = mesh.shape["chan"], mesh.shape["grp"]

    def body(*args):
        chans, tpl_count = args[0].shape[0], args[2].shape[0]
        if chans == 64 and tpl_count <= 32 and grp == 2:
            return packed(*args, chan, grp)
        return time_split(*args, chan, grp)

    in_specs = (
        P(None, ("parts", "chan", "grp")),
        P(),
        P("tpl", ("chan", "grp"), None),
        P("tpl", ("chan", "grp")),
        P("tpl", ("chan", "grp")),
        P(("chan", "grp")),
    )
    out_specs = P("tpl", ("parts", "chan"))
    return jax.shard_map(body, mesh=mesh, in_specs=in_specs, out_specs=out_specs, check_vma=False)
```
